128 devices in a mesh: row: 32 (over x, y, core), col: 4 (over z).
Axes of the slice: x: 4, y: 4, z: 4, core: 2. Of those that a mesh axis runs over, the one named last changes fastest.
Arguments:
- trailing: float32 [4096, 4096], P('row'), as said below
- inverse_rows: float32 [4096, 512], P('row')
- rhs_tail: float32 [4096, 2048], P('row', 'col'), may hold values from -6 to 6
- coupling: float32 [32768, 4096], P('row', 'col'), may hold values from -0.09375 to 0.09375
- rhs_head: float32 [32768, 2048], P('row', 'col'), may hold values from -6 to 6
- child_rows: int32 [64, 256], replicated, may hold values from 0 to 4095, as said below
- owner: int32 [64], replicated, may hold values from 0 to 31, as said below
Outputs:
- remaining: float32 [32768, 2048], P('row', 'col')
- solved: float32 [4096, 2048], P(None, 'col')
- handed: float32 [128, 256, 2048], P('row', None, 'col')
The draws below stay inside these ranges and needn't reach their ends.
Inputs may be any that keep to these rules, and one draw needn't show every extreme that they name: `trailing`: blocks of 512 x 512 on or below the block diagonal are zero. `child_rows`: each list holds 256 distinct rows in increasing order. `owner`: one subtree group owns exactly 4 child blocks, two groups own exactly one each, every other group owns two.
All inputs are finite; a program needn't handle non-finite values.
Results may differ from the reference program's by a relative error of at most 0.0001.
Values sent between devices are 32-bit elements; how exact they have to be, the bound alone decides.
No kernel may reach another device: no remote copies, remote signals or barrier semaphores. Data moves between devices by JAX's collectives and lax.ppermute only.
A program may use at most 128 MiB of HBM per device.

```python
import jax
import jax.numpy as jnp
from jax import lax

NB = 512
PANELS = 8
RHS = 2048
CROWS = 256
SLOTS = 4
W = 4096
NREST = 32768
CHILDREN = 64
N_ROW = 32


def draw_trailing(key, part):
    key = jax.random.fold_in(key, 11)
    upper = jnp.arange(W)[:, None] // NB < jnp.arange(W)[None, :] // NB
    values = jax.random.normal(key, (W, W), jnp.float32) * (0.5 / W ** 0.5)
    return jnp.where(upper, values, 0.0).astype(jnp.float32)


def draw_inverse_rows(key, part):
    key = jax.random.fold_in(key, 23)
    ident = (jnp.arange(W)[:, None] % NB == jnp.arange(NB)[None, :]).astype(jnp.float32)
    noise = jax.random.normal(key, (W, NB), jnp.float32) * (0.45 / NB ** 0.5)
    return (ident + noise).astype(jnp.float32)


def draw_child_rows(key, part):
    key = jax.random.fold_in(key, 37)
    keys = jax.random.split(key, CHILDREN)
    picks = jax.vmap(lambda k: jax.random.permutation(k, W)[:CROWS])(keys)
    picks = jnp.sort(picks, axis=1)
    picks = picks.at[0, 0].set(0).at[0, CROWS - 1].set(W - 1)
    return picks.astype(jnp.int32)


def draw_owner(key, part):
    key = jax.random.fold_in(key, 51)
    first, second = jax.random.split(key)
    groups = jax.random.permutation(first, N_ROW).astype(jnp.int32)
    order = jax.random.permutation(second, CHILDREN).astype(jnp.int32)
    position = jnp.arange(CHILDREN, dtype=jnp.int32)
    others = 1 + jnp.maximum(position - SLOTS, 0) % (N_ROW - 1)
    which = jnp.where(position < SLOTS, 0, others)
    values = groups[which]
    return jnp.zeros((CHILDREN,), jnp.int32).at[order].set(values)


def levels(own_key, dims, pieces, smallest, largest):
    loudness = 1.0
    for dim, shards_of in pieces:
        steps = jax.random.uniform(jax.random.fold_in(jax.random.fold_in(own_key, 6), dim), (shards_of,), jnp.float32, smallest / len(pieces), largest / len(pieces))
        loudness = loudness * jnp.repeat(jnp.exp(steps), dims[dim] // shards_of).reshape((-1,) + (1,) * (len(dims) - 1 - dim))
    return loudness


def gaussian(key, shape, deviation, reach, pieces=(), kind=jnp.bfloat16):
    array = jax.random.normal(key, shape, jnp.float32) * deviation
    if len(pieces) > 0:
        array = levels(key, shape, pieces, -0.22, 0.18) * array
    return jnp.clip(array, min=-reach, max=reach).astype(kind)


def setup_inputs(seed: int = 0) -> dict:
    arg_keys = jax.random.split(jax.random.key(seed), 8)
    trailing = draw_trailing(jax.random.fold_in(arg_keys[7], 71), 0)
    inverse_rows = draw_inverse_rows(jax.random.fold_in(arg_keys[7], 71), 0)
    rhs_tail = gaussian(arg_keys[2], (W, RHS), 1.0, 6.0, ((0, 32), (1, 4)), jnp.float32)
    coupling = gaussian(arg_keys[3], (NREST, W), W ** -0.5, 0.09375, ((0, 32), (1, 4)), jnp.float32)
    rhs_head = gaussian(arg_keys[4], (NREST, RHS), 1.0, 6.0, ((0, 32), (1, 4)), jnp.float32)
    child_rows = draw_child_rows(jax.random.fold_in(arg_keys[7], 71), 0)
    owner = draw_owner(jax.random.fold_in(arg_keys[7], 71), 0)
    return dict(trailing=trailing, inverse_rows=inverse_rows, rhs_tail=rhs_tail, coupling=coupling, rhs_head=rhs_head, child_rows=child_rows, owner=owner)


def reference(trailing, inverse_rows, rhs_tail, coupling, rhs_head, child_rows, owner):
    high = lax.Precision.HIGHEST
    solved = jnp.zeros((W, RHS), jnp.float32)
    for step in range(PANELS - 1, -1, -1):
        low = step * NB
        residual = rhs_tail[low:low + NB] - jnp.dot(trailing[low:low + NB], solved, precision=high)
        block = jnp.dot(inverse_rows[low:low + NB].T, residual, precision=high)
        solved = solved.at[low:low + NB].set(block)
    remaining = rhs_head - jnp.dot(coupling, solved, precision=high)
    onehot = (owner[:, None] == jnp.arange(N_ROW, dtype=jnp.int32)[None, :]).astype(jnp.int32)
    before = jnp.cumsum(onehot, axis=0) - onehot
    rank = jnp.sum(before * onehot, axis=1)
    target = (owner * SLOTS + rank).astype(jnp.int32)
    handed = jnp.zeros((N_ROW * SLOTS, CROWS, RHS), jnp.float32).at[target].set(solved[child_rows])
    return remaining, solved, handed
```

```python
import jax
import jax.numpy as jnp
from jax import lax
from jax.sharding import Mesh, PartitionSpec as P

SLOTS = 4
NX, NY, NC = 4, 4, 2
ROW = ("x", "y", "core")
SWAP = [(0, 1), (1, 0)]

highest = lax.Precision.HIGHEST
high = lax.Precision.HIGH


def mm(a, b):
    return jnp.dot(a, b, precision=highest)


def apply_inverse(inverse, residual):
    return lax.dot_general(inverse, residual, (((0,), (0,)), ((), ())), precision=highest)


def both_cores(own):
    return lax.ppermute(own, "core", SWAP)


def by_panel(own, other):
    rows, n = own.shape[1:]
    low = jnp.concatenate([own[0], own[1], other[0], other[1]], axis=0)
    hi = jnp.concatenate([own[2], own[3], other[2], other[3]], axis=0)
    return low, hi


def gather_y(piece, y):
    parts = [piece] + [lax.ppermute(piece, "y", [(i, i ^ s) for i in range(NY)]) for s in (1, 2, 3)]
    stack = jnp.stack(parts)
    return jnp.stack([lax.dynamic_index_in_dim(stack, y ^ j, 0, keepdims=False) for j in range(NY)])


def on_device(trailing, inverse_rows, rhs_tail, coupling, rhs_head, child_rows, owner):
    x = lax.axis_index("x")
    y = lax.axis_index("y")
    core = lax.axis_index("core")
    rows, window = trailing.shape
    width = inverse_rows.shape[1]
    columns = rhs_tail.shape[1]
    part = columns // NY
    pair = 2 * width

    gathered = lax.all_gather(coupling, "z", axis=0, tiled=False)

    t_diag = lax.dynamic_slice(trailing, (0, pair * x + width), (rows, width))
    t_next = lax.dynamic_slice(trailing, (0, pair * (x + 1)), (rows, pair))
    factors = jnp.concatenate([inverse_rows, t_diag], axis=1)
    right = rhs_tail.reshape(rows, NY, part).transpose(1, 0, 2)
    packed = jnp.concatenate([jnp.broadcast_to(factors, (NY,) + factors.shape), right], axis=2)
    packed = lax.all_to_all(packed, "y", split_axis=0, concat_axis=0, tiled=True)
    low, hi = by_panel(packed, both_cores(packed))
    g_low, g_hi = low[:, :width], hi[:, :width]
    t_mid = low[:, width : 2 * width]
    r_low, r_hi = low[:, 2 * width :], hi[:, 2 * width :]

    t_step = gather_y(t_next, y)
    t_step = jnp.concatenate(by_panel(t_step, both_cores(t_step)), axis=0)

    blocks = [None] * NX
    for p in range(NX - 1, -1, -1):
        x_hi = apply_inverse(g_hi, r_hi)
        x_low = apply_inverse(g_low, r_low - mm(t_mid, x_hi))
        mine = jnp.where(core == 0, x_low, x_hi)
        got = [lax.ppermute(mine, "x", [(p, (p + s) % NX)]) for s in (3, 1, 2)]
        mine = jnp.where(x == p, mine, got[0] + got[1] + got[2])
        if p > 0:
            other = both_cores(mine)
            block = jnp.concatenate([jnp.where(core == 0, mine, other), jnp.where(core == 0, other, mine)], axis=0)
            step = jnp.where(x == p - 1, mm(t_step, block), 0.0)
            r_low = r_low - step[:width]
            r_hi = r_hi - step[width:]
        full = gather_y(mine, y)
        full_other = both_cores(full)
        full = jnp.stack([jnp.where(core == 0, full, full_other), jnp.where(core == 0, full_other, full)])
        full = full.transpose(0, 2, 1, 3).reshape(pair, columns)
        blocks[p] = full
        if p > 1:
            far = mm(trailing[:, p * pair : (p + 1) * pair], full)
            far = jnp.where(x < p - 1, far, 0.0)
            far = far.reshape(rows, NY, part).transpose(1, 0, 2)
            far = lax.all_to_all(far, "y", split_axis=0, concat_axis=0, tiled=True)
            far_low, far_hi = by_panel(far, both_cores(far))
            r_low = r_low - far_low
            r_hi = r_hi - far_hi

    solved = jnp.concatenate(blocks, axis=0)
    remaining = rhs_head
    for p in range(NX):
        remaining = remaining - jnp.dot(gathered[p], blocks[p], precision=high)

    group = (x * NY + y) * NC + core
    owned = (owner == group).astype(jnp.int32)
    rank = jnp.cumsum(owned) - owned
    slot_ids = jnp.arange(SLOTS, dtype=jnp.int32)
    picked = (owned[None, :] == 1) & (rank[None, :] == slot_ids[:, None])
    rows_taken = jnp.sum(jnp.where(picked[:, :, None], child_rows[None, :, :], 0), axis=1)
    filled = jnp.any(picked, axis=1)
    handed = jnp.where(filled[:, None, None], solved[rows_taken], 0.0)
    return (remaining, solved, handed)


def solution(mesh):
    grid = Mesh(mesh.devices.reshape(NX, NY, NC, -1), ROW + ("z",))
    return jax.shard_map(
        on_device,
        mesh=grid,
        in_specs=(
            P(ROW, None),
            P(ROW, None),
            P(ROW, "z"),
            P(ROW, "z"),
            P(ROW, "z"),
            P(),
            P(),
        ),
        out_specs=(P(ROW, "z"), P(None, "z"), P(ROW, None, "z")),
        check_vma=False,
    )
```

```python
import functools

import jax
import jax.numpy as jnp
from jax import lax
from jax.experimental import pallas as pl
from jax.experimental.pallas import tpu as pltpu
from jax.sharding import Mesh, PartitionSpec as P

SLOTS = 4
NX, NY, NC = 4, 4, 2
ROW = ("x", "y", "core")
SWAP = [(0, 1), (1, 0)]
MIB = 1024 * 1024

highest = lax.Precision.HIGHEST


def mm(a, b):
    return jnp.dot(a, b, precision=highest, preferred_element_type=jnp.float32)


def mm_t(a, b):
    return lax.dot_general(a, b, (((0,), (0,)), ((), ())), precision=highest, preferred_element_type=jnp.float32)


def split(a):
    top = a.astype(jnp.bfloat16)
    return top, (a - top.astype(jnp.float32)).astype(jnp.bfloat16)


def mm3(a_top, a_low, b_top, b_low):
    one = functools.partial(jnp.dot, preferred_element_type=jnp.float32)
    return one(a_top, b_top) + (one(a_low, b_top) + one(a_top, b_low))


def both_cores(own):
    return lax.ppermute(own, "core", SWAP)


def exchange_y(piece, axis=0):
    one, three = [[(i, i ^ s) for i in range(NY)] for s in (1, 3)]
    n = piece.shape[axis] // 2
    a = lax.ppermute(piece, "y", one)
    b = lax.ppermute(piece, "y", three)
    c = lax.ppermute(lax.slice_in_dim(b, 0, n, axis=axis), "y", one)
    d = lax.ppermute(lax.slice_in_dim(a, n, 2 * n, axis=axis), "y", three)
    return a, b, c, d


def solve_kernel(idx, fac_own, fac_other, r_own, r_other, out, g_hi, t_mid, g_low, sems):
    width = g_hi.shape[-1]
    core = idx[2]
    copies = []
    for n, (dst, y0, col) in enumerate(((g_hi, 2, 0), (t_mid, 0, width), (g_low, 0, 0))):
        for j, fac in enumerate((fac_own, fac_other)):
            cp = pltpu.make_async_copy(fac.at[pl.ds(y0, 2), :, pl.ds(col, width)], dst.at[j], sems.at[2 * n + j])
            cp.start()
            copies.append(cp)

    def rows(y0):
        a = r_own[pl.ds(y0, 2)]
        b = r_other[pl.ds(y0, 2)]
        return jnp.concatenate([a.reshape(-1, a.shape[-1]), b.reshape(-1, b.shape[-1])], axis=0)

    r_hi, r_low = rows(2), rows(0)
    copies[0].wait()
    copies[1].wait()
    x_hi = mm_t(g_hi[...].reshape(width, width), r_hi)
    copies[2].wait()
    copies[3].wait()
    r_low = r_low - mm(t_mid[...].reshape(width, width), x_hi)
    copies[4].wait()
    copies[5].wait()
    x_low = mm_t(g_low[...].reshape(width, width), r_low)
    out[...] = jnp.where(core == 0, x_low, x_hi)


def solve(idx, packed, packed_other, r_own, r_other, width):
    part = r_own.shape[-1]
    vmem = pl.BlockSpec(memory_space=pltpu.VMEM)
    hbm = pl.BlockSpec(memory_space=pl.ANY)
    half = pltpu.VMEM((2, 2, width // 4, width), jnp.float32)
    return pl.pallas_call(
        solve_kernel,
        out_shape=jax.ShapeDtypeStruct((width, part), jnp.float32),
        in_specs=[pl.BlockSpec(memory_space=pltpu.SMEM), hbm, hbm, vmem, vmem],
        out_specs=vmem,
        scratch_shapes=[half, half, half, pltpu.SemaphoreType.DMA((6,))],
        compiler_params=pltpu.CompilerParams(vmem_limit_bytes=24 * MIB),
        cost_estimate=pl.CostEstimate(flops=1000, bytes_accessed=1000, transcendentals=0),
        name="solve_pair",
    )(idx, packed, packed_other, r_own, r_other)


def update_kernel(p, idx, mine, other, r_own, trailing, near, far, top, bottom, out, t_buf, sems):
    x, y, core = idx[0], idx[1], idx[2]
    ny, rows, pair = t_buf.shape
    half = rows // 2
    moves = (
        (trailing.at[:, pl.ds(p * pair, pair)], t_buf.at[y]),
        (near, t_buf.at[y ^ 1]),
        (far, t_buf.at[y ^ 3]),
        (top, t_buf.at[y ^ 2, pl.ds(0, half)]),
        (bottom, t_buf.at[y ^ 2, pl.ds(half, half)]),
    )
    copies = [pltpu.make_async_copy(src, dst, sems.at[n]) for n, (src, dst) in enumerate(moves)]
    for cp in copies:
        cp.start()
    first = jnp.where(core == 0, mine[...], other[...])
    second = jnp.where(core == 0, other[...], mine[...])
    block = jnp.concatenate([first, second], axis=0)
    for cp in copies:
        cp.wait()
    step = mm(t_buf[...].reshape(ny * rows, pair), block).reshape(r_own.shape)
    out[...] = jnp.where(x < p, r_own[...] - step, r_own[...])


def update(p, idx, mine, other, r_own, trailing, pieces):
    vmem = pl.BlockSpec(memory_space=pltpu.VMEM)
    hbm = pl.BlockSpec(memory_space=pl.ANY)
    rows, pair = pieces[0].shape
    return pl.pallas_call(
        functools.partial(update_kernel, p),
        out_shape=jax.ShapeDtypeStruct(r_own.shape, jnp.float32),
        in_specs=[pl.BlockSpec(memory_space=pltpu.SMEM), vmem, vmem, vmem] + [hbm] * 5,
        out_specs=vmem,
        scratch_shapes=[pltpu.VMEM((NY, rows, pair), jnp.float32), pltpu.SemaphoreType.DMA((5,))],
        compiler_params=pltpu.CompilerParams(vmem_limit_bytes=24 * MIB),
        cost_estimate=pl.CostEstimate(flops=1000, bytes_accessed=1000, transcendentals=0),
        name="update_rows",
    )(idx, mine, other, r_own, trailing, *pieces)


def join_kernel(idx, own, near, far, top, bottom, out, sems):
    y = idx[1]
    height, part = own.shape[1:]
    half = height // 2

    def columns(s):
        return pl.ds(pl.multiple_of((y ^ s) * part, part), part)

    moves = (
        (own, out.at[:, :, columns(0)]),
        (near, out.at[:, :, columns(1)]),
        (far, out.at[:, :, columns(3)]),
        (top, out.at[:, pl.ds(0, half), columns(2)]),
        (bottom, out.at[:, pl.ds(half, half), columns(2)]),
    )
    copies = [pltpu.make_async_copy(src, dst, sems.at[n]) for n, (src, dst) in enumerate(moves)]
    for cp in copies:
        cp.start()
    for cp in copies:
        cp.wait()


def join(idx, own, pieces):
    n, height, part = own.shape
    hbm = pl.BlockSpec(memory_space=pl.ANY)
    return pl.pallas_call(
        join_kernel,
        grid=(1,),
        out_shape=jax.ShapeDtypeStruct((n, height, NY * part), jnp.float32),
        in_specs=[pl.BlockSpec(memory_space=pltpu.SMEM)] + [hbm] * 5,
        out_specs=pl.BlockSpec((n, height, NY * part), lambda i: (0, 0, 0)),
        scratch_shapes=[pltpu.SemaphoreType.DMA((5,))],
        compiler_params=pltpu.CompilerParams(vmem_limit_bytes=24 * MIB),
        cost_estimate=pl.CostEstimate(flops=0, bytes_accessed=1000, transcendentals=0),
        name="join_columns",
    )(idx, own, *pieces)


def assemble_kernel(idx, own, other, *refs):
    core = idx[2]
    out, top, low = refs[-3:]
    height = own.shape[1]
    for panel in range(2):
        value = jnp.where(core == panel, own[0], other[0])
        rows = pl.ds(panel * height, height)
        out[rows] = value
        top[0, rows], low[0, rows] = split(value)


def assemble(idx, first, own, other, solved):
    n, height, columns = own.shape
    hbm = pl.BlockSpec(memory_space=pl.ANY)
    block = pl.BlockSpec((1, height, columns), lambda i: (i, 0, 0))
    terms = pl.BlockSpec((1, 2 * height, columns), lambda i: (i, 0, 0))
    term = jax.ShapeDtypeStruct((n, 2 * height, columns), jnp.bfloat16)
    return pl.pallas_call(
        assemble_kernel,
        grid=(n,),
        out_shape=[jax.ShapeDtypeStruct((NX * 2 * height, columns), jnp.float32), term, term],
        in_specs=[pl.BlockSpec(memory_space=pltpu.SMEM), block, block] + [hbm] * len(solved),
        out_specs=[pl.BlockSpec((2 * height, columns), lambda i: (first + i, 0)), terms, terms],
        input_output_aliases={3: 0} if solved else {},
        compiler_params=pltpu.CompilerParams(vmem_limit_bytes=32 * MIB),
        cost_estimate=pl.CostEstimate(flops=0, bytes_accessed=n * 6 * MIB, transcendentals=0),
        name="assemble_pairs",
    )(idx, own, other, *solved)


def product_kernel(start, c, b_top, b_low, out):
    @pl.when(pl.program_id(1) == 0)
    def _():
        out[...] = start[...]

    a_top, a_low = split(c[0])
    out[...] -= mm3(a_top, a_low, b_top[0], b_low[0])


def product(start, blocks, top, low, first):
    rows, columns = start.shape
    count, pair, _ = top.shape
    tile = rows // 2
    whole = pl.BlockSpec((tile, columns), lambda i, j: (i, 0))
    term = pl.BlockSpec((1, pair, columns), lambda i, j: (j, 0, 0))
    return pl.pallas_call(
        product_kernel,
        grid=(rows // tile, count),
        out_shape=jax.ShapeDtypeStruct(start.shape, jnp.float32),
        in_specs=[whole, pl.BlockSpec((1, tile, pair), lambda i, j: (first + j, i, 0)), term, term],
        out_specs=whole,
        compiler_params=pltpu.CompilerParams(vmem_limit_bytes=40 * MIB),
        cost_estimate=pl.CostEstimate(
            flops=6 * rows * pair * columns * count, bytes_accessed=count * 8 * MIB, transcendentals=0
        ),
        name="product",
    )(start, blocks, top, low)


def hand_kernel(filled, taken, solved, out):
    slot = pl.program_id(0)
    count = out.shape[1]

    @pl.when(filled[slot] == 1)
    def _():
        def body(n, carry):
            for u in range(8):
                i = n * 8 + u
                out[0, pl.ds(i, 1)] = solved[pl.ds(taken[slot, i], 1)]
            return carry

        lax.fori_loop(0, count // 8, body, 0)

    @pl.when(filled[slot] == 0)
    def _():
        out[...] = jnp.zeros_like(out)


def hand(filled, taken, solved):
    slots, count = taken.shape
    columns = solved.shape[1]
    smem = pl.BlockSpec(memory_space=pltpu.SMEM)
    return pl.pallas_call(
        hand_kernel,
        grid=(slots,),
        out_shape=jax.ShapeDtypeStruct((slots, count, columns), jnp.float32),
        in_specs=[smem, smem, pl.BlockSpec(solved.shape, lambda i: (0, 0))],
        out_specs=pl.BlockSpec((1, count, columns), lambda i: (i, 0, 0)),
        compiler_params=pltpu.CompilerParams(vmem_limit_bytes=32 * MIB),
        cost_estimate=pl.CostEstimate(flops=0, bytes_accessed=10 * MIB, transcendentals=0),
        name="hand_down",
    )(filled, taken, solved)


def on_device(trailing, inverse_rows, rhs_tail, coupling, rhs_head, child_rows, owner):
    x = lax.axis_index("x")
    y = lax.axis_index("y")
    core = lax.axis_index("core")
    z = lax.axis_index("z")
    idx = jnp.stack([x, y, core, z]).astype(jnp.int32)
    rows, window = trailing.shape
    width = inverse_rows.shape[1]
    columns = rhs_tail.shape[1]
    part = columns // NY
    pair = 2 * width

    gathered = lax.all_gather(coupling, "z", axis=0, tiled=False)

    t_diag = lax.dynamic_slice(trailing, (0, pair * x + width), (rows, width))
    factors = jnp.concatenate([inverse_rows, t_diag], axis=1)
    right = rhs_tail.reshape(rows, NY, part).transpose(1, 0, 2)
    packed = jnp.concatenate([jnp.broadcast_to(factors, (NY,) + factors.shape), right], axis=2)
    packed = lax.all_to_all(packed, "y", split_axis=0, concat_axis=0, tiled=True)
    packed_other = both_cores(packed)
    r_own = packed[:, :, pair:]
    r_other = packed_other[:, :, pair:]

    chunks = {}
    after = packed
    for q in range(NX - 1, 0, -1):
        piece, _ = lax.optimization_barrier((trailing[:, q * pair : (q + 1) * pair], after))
        chunks[q] = exchange_y(piece)
        after = chunks[q][:2]

    halves = [None] * NX
    for p in range(NX - 1, -1, -1):
        mine = solve(idx, packed, packed_other, r_own, r_other, width)
        got = [lax.ppermute(mine, "x", [(p, (p + s) % NX)]) for s in (3, 1, 2)]
        halves[p] = jnp.where(x == p, mine, got[0] + got[1] + got[2])
        if p > 0:
            other = both_cores(halves[p])
            r_own = update(p, idx, halves[p], other, r_own, trailing, chunks[p])
            r_other = both_cores(r_own)
        if p == 2:
            first, _ = lax.optimization_barrier((halves[2:], r_own))
            first = jnp.stack(first)
            first_pieces = exchange_y(first, axis=1)
        if p == 1:
            second, _ = lax.optimization_barrier((halves[1][None], r_own))
            second_pieces = exchange_y(second, axis=1)
    first_pieces, second_pieces, last = lax.optimization_barrier((first_pieces, second_pieces, halves[0][None]))
    last_pieces = exchange_y(last, axis=1)
    first = join(idx, first, first_pieces)
    solved, top, low = assemble(idx, 2, first, both_cores(first), ())
    remaining = product(rhs_head, gathered, top, low, 2)
    second = join(idx, second, second_pieces)
    solved, top, low = assemble(idx, 1, second, both_cores(second), (solved,))
    remaining = product(remaining, gathered, top, low, 1)
    last_pieces, remaining = lax.optimization_barrier((last_pieces, remaining))
    last = join(idx, last, last_pieces)
    solved, top, low = assemble(idx, 0, last, both_cores(last), (solved,))
    remaining = product(remaining, gathered, top, low, 0)

    group = (x * NY + y) * NC + core
    owned = (owner == group).astype(jnp.int32)
    rank = jnp.cumsum(owned) - owned
    slot_ids = jnp.arange(SLOTS, dtype=jnp.int32)
    picked = (owned[None, :] == 1) & (rank[None, :] == slot_ids[:, None])
    rows_taken = jnp.sum(jnp.where(picked[:, :, None], child_rows[None, :, :], 0), axis=1)
    filled = jnp.any(picked, axis=1)
    handed = hand(filled.astype(jnp.int32), rows_taken, solved)
    return (remaining, solved, handed)


def solution(mesh):
    grid = Mesh(mesh.devices.reshape(NX, NY, NC, -1), ROW + ("z",))
    return jax.shard_map(
        on_device,
        mesh=grid,
        in_specs=(
            P(ROW, None),
            P(ROW, None),
            P(ROW, "z"),
            P(ROW, "z"),
            P(ROW, "z"),
            P(),
            P(),
        ),
        out_specs=(P(ROW, "z"), P(None, "z"), P(ROW, None, "z")),
        check_vma=False,
    )
```

```python
import functools

import jax
import jax.numpy as jnp
from jax import lax
from jax.experimental import pallas as pl
from jax.experimental.pallas import tpu as pltpu
from jax.sharding import Mesh, PartitionSpec as P

SLOTS = 4
NX, NY, NC = 4, 4, 2
ROW = ("x", "y", "core")
SWAP = [(0, 1), (1, 0)]
MIB = 1024 * 1024

def three_terms(a):
    top = a.astype(jnp.bfloat16)
    rest = a - top.astype(jnp.float32)
    mid = rest.astype(jnp.bfloat16)
    return top, mid, (rest - mid.astype(jnp.float32)).astype(jnp.bfloat16)


def mm(a, b, a_axis=1):
    n = b.shape[1]
    top, mid, low = three_terms(a)
    terms = jnp.concatenate(three_terms(b), axis=1)

    def dot(u, v):
        return lax.dot_general(u, v, (((a_axis,), (0,)), ((), ())), preferred_element_type=jnp.float32)

    first = dot(top, terms)
    second = dot(mid, terms[:, : 2 * n])
    third = dot(low, terms[:, :n])
    small = first[:, 2 * n :] + second[:, n:] + third
    return first[:, :n] + ((first[:, n : 2 * n] + second[:, :n]) + small)


def mm_t(a, b):
    return mm(a, b, 0)


def split(a):
    top = a.astype(jnp.bfloat16)
    return top, (a - top.astype(jnp.float32)).astype(jnp.bfloat16)


def mm3(a_top, a_low, b_top, b_low):
    one = functools.partial(jnp.dot, preferred_element_type=jnp.float32)
    return one(a_top, b_top) + (one(a_low, b_top) + one(a_top, b_low))


def both_cores(own):
    return lax.ppermute(own, "core", SWAP)


ONE, THREE = [[(i, i ^ s) for i in range(NY)] for s in (1, 3)]


def neighbours_y(piece):
    return lax.ppermute(piece, "y", ONE), lax.ppermute(piece, "y", THREE)


def pass_on_y(a, b, axis):
    n = a.shape[axis] // 2
    c = lax.ppermute(lax.slice_in_dim(b, 0, n, axis=axis), "y", ONE)
    d = lax.ppermute(lax.slice_in_dim(a, n, 2 * n, axis=axis), "y", THREE)
    return a, b, c, d


def exchange_y(piece, axis=0):
    return pass_on_y(*neighbours_y(piece), axis)


def solve_kernel(p, idx, fac_own, fac_other, r_own, r_other, out, g_hi, t_mid, g_low, sems):
    @pl.when(idx[0] == p)
    def _():
        width = g_hi.shape[-1]
        copies = []
        for n, (dst, y0, col) in enumerate(((g_hi, 2, 0), (t_mid, 0, width), (g_low, 0, 0))):
            for j, fac in enumerate((fac_own, fac_other)):
                src = fac.at[pl.ds(y0, 2), :, pl.ds(col, width)]
                cp = pltpu.make_async_copy(src, dst.at[j], sems.at[2 * n + j])
                cp.start()
                copies.append(cp)

        def rows(y0):
            a = r_own[pl.ds(y0, 2)]
            b = r_other[pl.ds(y0, 2)]
            return jnp.concatenate([a.reshape(-1, a.shape[-1]), b.reshape(-1, b.shape[-1])], axis=0)

        r_hi, r_low = rows(2), rows(0)
        copies[0].wait()
        copies[1].wait()
        x_hi = mm_t(g_hi[...].reshape(width, width), r_hi)
        copies[2].wait()
        copies[3].wait()
        r_low = r_low - mm(t_mid[...].reshape(width, width), x_hi)
        copies[4].wait()
        copies[5].wait()
        x_low = mm_t(g_low[...].reshape(width, width), r_low)
        out[...] = jnp.where(idx[2] == 0, x_low, x_hi)


def solve(p, idx, packed, packed_other, r_own, r_other, width):
    part = r_own.shape[-1]
    vmem = pl.BlockSpec(memory_space=pltpu.VMEM)
    hbm = pl.BlockSpec(memory_space=pltpu.HBM)
    half = pltpu.VMEM((2, 2, width // 4, width), jnp.float32)
    return pl.pallas_call(
        functools.partial(solve_kernel, p),
        out_shape=jax.ShapeDtypeStruct((width, part), jnp.float32),
        in_specs=[pl.BlockSpec(memory_space=pltpu.SMEM), hbm, hbm, vmem, vmem],
        out_specs=vmem,
        scratch_shapes=[half, half, half, pltpu.SemaphoreType.DMA((6,))],
        compiler_params=pltpu.CompilerParams(vmem_limit_bytes=24 * MIB),
        cost_estimate=pl.CostEstimate(flops=1000, bytes_accessed=1000, transcendentals=0),
        name="solve_pair",
    )(idx, packed, packed_other, r_own, r_other)


def update_kernel(p, idx, mine, other, r_own, trailing, near, far, top, bottom, out, t_buf, sems):
    x, y, core = idx[0], idx[1], idx[2]
    ny, rows, pair = t_buf.shape
    half = rows // 2
    moves = (
        (trailing.at[:, pl.ds(p * pair, pair)], t_buf.at[y]),
        (near, t_buf.at[y ^ 1]),
        (far, t_buf.at[y ^ 3]),
        (top, t_buf.at[y ^ 2, pl.ds(0, half)]),
        (bottom, t_buf.at[y ^ 2, pl.ds(half, half)]),
    )

    @pl.when(x >= p)
    def _():
        out[...] = r_own[...]

    @pl.when(x < p)
    def _():
        copies = [pltpu.make_async_copy(src, dst, sems.at[n]) for n, (src, dst) in enumerate(moves)]
        for cp in copies:
            cp.start()
        first = jnp.where(core == 0, mine[...], other[...])
        second = jnp.where(core == 0, other[...], mine[...])
        block = jnp.concatenate([first, second], axis=0)
        for cp in copies:
            cp.wait()
        step = mm(t_buf[...].reshape(ny * rows, pair), block).reshape(r_own.shape)
        out[...] = r_own[...] - step


def update(p, idx, mine, other, r_own, trailing, pieces):
    vmem = pl.BlockSpec(memory_space=pltpu.VMEM)
    hbm = pl.BlockSpec(memory_space=pltpu.HBM)
    rows, pair = pieces[0].shape
    return pl.pallas_call(
        functools.partial(update_kernel, p),
        out_shape=jax.ShapeDtypeStruct(r_own.shape, jnp.float32),
        in_specs=[pl.BlockSpec(memory_space=pltpu.SMEM), vmem, vmem, vmem] + [hbm] * 5,
        out_specs=vmem,
        scratch_shapes=[pltpu.VMEM((NY, rows, pair), jnp.float32), pltpu.SemaphoreType.DMA((5,))],
        compiler_params=pltpu.CompilerParams(vmem_limit_bytes=24 * MIB),
        cost_estimate=pl.CostEstimate(flops=1000, bytes_accessed=1000, transcendentals=0),
        name="update_rows",
    )(idx, mine, other, r_own, trailing, *pieces)


def join_kernel(idx, own, near, far, top, bottom, out, sems):
    y = idx[1]
    height, part = own.shape[1:]
    half = height // 2

    def columns(s):
        return pl.ds(pl.multiple_of((y ^ s) * part, part), part)

    moves = (
        (own, out.at[:, :, columns(0)]),
        (near, out.at[:, :, columns(1)]),
        (far, out.at[:, :, columns(3)]),
        (top, out.at[:, pl.ds(0, half), columns(2)]),
        (bottom, out.at[:, pl.ds(half, half), columns(2)]),
    )
    copies = [pltpu.make_async_copy(src, dst, sems.at[n]) for n, (src, dst) in enumerate(moves)]
    for cp in copies:
        cp.start()
    for cp in copies:
        cp.wait()


def join(idx, own, pieces):
    n, height, part = own.shape
    hbm = pl.BlockSpec(memory_space=pltpu.HBM)
    return pl.pallas_call(
        join_kernel,
        grid=(1,),
        out_shape=jax.ShapeDtypeStruct((n, height, NY * part), jnp.float32),
        in_specs=[pl.BlockSpec(memory_space=pltpu.SMEM)] + [hbm] * 5,
        out_specs=pl.BlockSpec((n, height, NY * part), lambda i: (0, 0, 0)),
        scratch_shapes=[pltpu.SemaphoreType.DMA((5,))],
        compiler_params=pltpu.CompilerParams(vmem_limit_bytes=24 * MIB),
        cost_estimate=pl.CostEstimate(flops=0, bytes_accessed=n * 3 * MIB, transcendentals=0),
        name="join_columns",
    )(idx, own, *pieces)


def assemble_kernel(idx, own, other, *refs):
    core = idx[2]
    out, top, low = refs[-3:]
    height = own.shape[1]
    for panel in range(2):
        value = jnp.where(core == panel, own[0], other[0])
        rows = pl.ds(panel * height, height)
        out[rows] = value
        top[0, rows], low[0, rows] = split(value)


def assemble(idx, first, own, other, solved):
    n, height, columns = own.shape
    hbm = pl.BlockSpec(memory_space=pltpu.HBM)
    block = pl.BlockSpec((1, height, columns), lambda i: (i, 0, 0))
    terms = pl.BlockSpec((1, 2 * height, columns), lambda i: (i, 0, 0))
    term = jax.ShapeDtypeStruct((n, 2 * height, columns), jnp.bfloat16)
    return pl.pallas_call(
        assemble_kernel,
        grid=(n,),
        out_shape=[jax.ShapeDtypeStruct((NX * 2 * height, columns), jnp.float32), term, term],
        in_specs=[pl.BlockSpec(memory_space=pltpu.SMEM), block, block] + [hbm] * len(solved),
        out_specs=[pl.BlockSpec((2 * height, columns), lambda i: (first + i, 0)), terms, terms],
        input_output_aliases={3: 0} if solved else {},
        compiler_params=pltpu.CompilerParams(vmem_limit_bytes=32 * MIB),
        cost_estimate=pl.CostEstimate(flops=0, bytes_accessed=n * 6 * MIB, transcendentals=0),
        name="assemble_pairs",
    )(idx, own, other, *solved)


def product_kernel(start, c, b_top, b_low, out):
    @pl.when(pl.program_id(1) == 0)
    def _():
        out[...] = start[...]

    a_top, a_low = split(c[0])
    out[...] -= mm3(a_top, a_low, b_top[0], b_low[0])


def product(start, blocks, top, low, first):
    rows, columns = start.shape
    count, pair, _ = top.shape
    tile = rows // (4 if count == 1 else 2)
    whole = pl.BlockSpec((tile, columns), lambda i, j: (i, 0))
    term = pl.BlockSpec((1, pair, columns), lambda i, j: (j, 0, 0))
    return pl.pallas_call(
        product_kernel,
        grid=(rows // tile, count),
        out_shape=jax.ShapeDtypeStruct(start.shape, jnp.float32),
        in_specs=[whole, pl.BlockSpec((1, tile, pair), lambda i, j: (first + j, i, 0)), term, term],
        out_specs=whole,
        compiler_params=pltpu.CompilerParams(vmem_limit_bytes=40 * MIB),
        cost_estimate=pl.CostEstimate(
            flops=6 * rows * pair * columns * count, bytes_accessed=count * 8 * MIB, transcendentals=0
        ),
        name="product",
    )(start, blocks, top, low)


def hand_kernel(filled, taken, solved, out):
    slot = pl.program_id(0)
    count = out.shape[1]

    @pl.when(filled[slot] == 1)
    def _():
        def body(n, carry):
            for u in range(8):
                i = n * 8 + u
                out[0, pl.ds(i, 1)] = solved[pl.ds(taken[slot, i], 1)]
            return carry

        lax.fori_loop(0, count // 8, body, 0)

    @pl.when(filled[slot] == 0)
    def _():
        out[...] = jnp.zeros_like(out)


def hand(filled, taken, solved):
    slots, count = taken.shape
    columns = solved.shape[1]
    smem = pl.BlockSpec(memory_space=pltpu.SMEM)
    return pl.pallas_call(
        hand_kernel,
        grid=(slots,),
        out_shape=jax.ShapeDtypeStruct((slots, count, columns), jnp.float32),
        in_specs=[smem, smem, pl.BlockSpec(solved.shape, lambda i: (0, 0))],
        out_specs=pl.BlockSpec((1, count, columns), lambda i: (i, 0, 0)),
        compiler_params=pltpu.CompilerParams(vmem_limit_bytes=32 * MIB),
        cost_estimate=pl.CostEstimate(flops=0, bytes_accessed=10 * MIB, transcendentals=0),
        name="hand_down",
    )(filled, taken, solved)


def on_device(trailing, inverse_rows, rhs_tail, coupling, rhs_head, child_rows, owner):
    x = lax.axis_index("x")
    y = lax.axis_index("y")
    core = lax.axis_index("core")
    z = lax.axis_index("z")
    idx = jnp.stack([x, y, core, z]).astype(jnp.int32)
    rows, window = trailing.shape
    width = inverse_rows.shape[1]
    columns = rhs_tail.shape[1]
    part = columns // NY
    pair = 2 * width

    gathered = lax.all_gather(coupling, "z", axis=0, tiled=False)

    t_diag = lax.dynamic_slice(trailing, (0, pair * x + width), (rows, width))
    factors = jnp.concatenate([inverse_rows, t_diag], axis=1)
    right = rhs_tail.reshape(rows, NY, part).transpose(1, 0, 2)
    packed = jnp.concatenate([jnp.broadcast_to(factors, (NY,) + factors.shape), right], axis=2)
    packed = lax.all_to_all(packed, "y", split_axis=0, concat_axis=0, tiled=True)
    packed_other = both_cores(packed)
    r_own = packed[:, :, pair:]
    r_other = packed_other[:, :, pair:]

    chunks = {}
    after = packed
    for q in range(NX - 1, 0, -1):
        piece, _ = lax.optimization_barrier((trailing[:, q * pair : (q + 1) * pair], after))
        chunks[q] = exchange_y(piece)
        after = chunks[q][:2]

    halves = [None] * NX
    for p in range(NX - 1, -1, -1):
        mine = solve(p, idx, packed, packed_other, r_own, r_other, width)
        got = [lax.ppermute(mine, "x", [(p, (p + s) % NX)]) for s in (2, 3, 1)]
        halves[p] = jnp.where(x == p, mine, got[0] + got[1] + got[2])
        if p > 0:
            other = both_cores(halves[p])
            r_own = update(p, idx, halves[p], other, r_own, trailing, chunks[p])
            r_other = both_cores(r_own)
        if p == 2:
            first, _ = lax.optimization_barrier((halves[2:], r_own))
            first = jnp.stack(first)
            first_pieces = exchange_y(first, axis=1)
        if p == 1:
            second, _ = lax.optimization_barrier((halves[1][None], r_own))
            second_pieces = exchange_y(second, axis=1)
    first_pieces, second_pieces, last = lax.optimization_barrier((first_pieces, second_pieces, halves[0][None]))
    last_pieces = neighbours_y(last)
    first = join(idx, first, first_pieces)
    solved, top, low = assemble(idx, 2, first, both_cores(first), ())
    second = join(idx, second, second_pieces)
    solved, top2, low2 = assemble(idx, 1, second, both_cores(second), (solved,))
    top, last_pieces = lax.optimization_barrier((top, last_pieces))
    last_pieces = pass_on_y(*last_pieces, 1)
    remaining = product(rhs_head, gathered, top, low, 2)
    remaining = product(remaining, gathered, top2, low2, 1)
    last_pieces, remaining = lax.optimization_barrier((last_pieces, remaining))
    last = join(idx, last, last_pieces)
    solved, top, low = assemble(idx, 0, last, both_cores(last), (solved,))
    remaining = product(remaining, gathered, top, low, 0)

    group = (x * NY + y) * NC + core
    owned = (owner == group).astype(jnp.int32)
    rank = jnp.cumsum(owned) - owned
    slot_ids = jnp.arange(SLOTS, dtype=jnp.int32)
    picked = (owned[None, :] == 1) & (rank[None, :] == slot_ids[:, None])
    rows_taken = jnp.sum(jnp.where(picked[:, :, None], child_rows[None, :, :], 0), axis=1)
    filled = jnp.any(picked, axis=1)
    handed = hand(filled.astype(jnp.int32), rows_taken, solved)
    return (remaining, solved, handed)


def solution(mesh):
    grid = Mesh(mesh.devices.reshape(NX, NY, NC, -1), ROW + ("z",))
    return jax.shard_map(
        on_device,
        mesh=grid,
        in_specs=(
            P(ROW, None),
            P(ROW, None),
            P(ROW, "z"),
            P(ROW, "z"),
            P(ROW, "z"),
            P(),
            P(),
        ),
        out_specs=(P(ROW, "z"), P(None, "z"), P(ROW, None, "z")),
        check_vma=False,
    )
```

```python
import functools

import jax
import jax.numpy as jnp
from jax import lax
from jax.experimental import pallas as pl
from jax.experimental.pallas import tpu as pltpu
from jax.sharding import Mesh, PartitionSpec as P

SLOTS = 4
NX, NY, NC = 4, 4, 2
ROW = ("x", "y", "core")
SWAP = [(0, 1), (1, 0)]
MIB = 1024 * 1024

def three_terms(a):
    top = a.astype(jnp.bfloat16)
    rest = a - top.astype(jnp.float32)
    mid = rest.astype(jnp.bfloat16)
    return top, mid, (rest - mid.astype(jnp.float32)).astype(jnp.bfloat16)


def mm(a, b, a_axis=1):
    n = b.shape[1]
    top, mid, low = three_terms(a)
    terms = jnp.concatenate(three_terms(b), axis=1)

    def dot(u, v):
        return lax.dot_general(u, v, (((a_axis,), (0,)), ((), ())), preferred_element_type=jnp.float32)

    first = dot(top, terms)
    second = dot(mid, terms[:, : 2 * n])
    third = dot(low, terms[:, :n])
    small = first[:, 2 * n :] + second[:, n:] + third
    return first[:, :n] + ((first[:, n : 2 * n] + second[:, :n]) + small)


def mm_t(a, b):
    return mm(a, b, 0)


def split(a):
    top = a.astype(jnp.bfloat16)
    return top, (a - top.astype(jnp.float32)).astype(jnp.bfloat16)


def mm3(a_top, a_low, b_top, b_low):
    one = functools.partial(jnp.dot, preferred_element_type=jnp.float32)
    return one(a_top, b_top) + (one(a_low, b_top) + one(a_top, b_low))


def both_cores(own):
    return lax.ppermute(own, "core", SWAP)


ONE, THREE = [[(i, i ^ s) for i in range(NY)] for s in (1, 3)]


def neighbours_y(piece):
    return lax.ppermute(piece, "y", ONE), lax.ppermute(piece, "y", THREE)


def pass_on_y(a, b, axis):
    n = a.shape[axis] // 2
    c = lax.ppermute(lax.slice_in_dim(b, 0, n, axis=axis), "y", ONE)
    d = lax.ppermute(lax.slice_in_dim(a, n, 2 * n, axis=axis), "y", THREE)
    return a, b, c, d


def exchange_y(piece, axis=0):
    return pass_on_y(*neighbours_y(piece), axis)


def solve_kernel(p, idx, fac_own, fac_other, r_own, r_other, out, g_hi, t_mid, g_low, sems):
    @pl.when(idx[0] == p)
    def _():
        width = g_hi.shape[-1]
        copies = []
        for n, (dst, y0, col) in enumerate(((g_hi, 2, 0), (t_mid, 0, width), (g_low, 0, 0))):
            for j, fac in enumerate((fac_own, fac_other)):
                src = fac.at[pl.ds(y0, 2), :, pl.ds(col, width)]
                cp = pltpu.make_async_copy(src, dst.at[j], sems.at[2 * n + j])
                cp.start()
                copies.append(cp)

        def rows(y0):
            a = r_own[pl.ds(y0, 2)]
            b = r_other[pl.ds(y0, 2)]
            return jnp.concatenate([a.reshape(-1, a.shape[-1]), b.reshape(-1, b.shape[-1])], axis=0)

        r_hi, r_low = rows(2), rows(0)
        copies[0].wait()
        copies[1].wait()
        x_hi = mm_t(g_hi[...].reshape(width, width), r_hi)
        copies[2].wait()
        copies[3].wait()
        r_low = r_low - mm(t_mid[...].reshape(width, width), x_hi)
        copies[4].wait()
        copies[5].wait()
        x_low = mm_t(g_low[...].reshape(width, width), r_low)
        out[...] = jnp.where(idx[2] == 0, x_low, x_hi)


def solve(p, idx, packed, packed_other, r_own, r_other, width):
    part = r_own.shape[-1]
    vmem = pl.BlockSpec(memory_space=pltpu.VMEM)
    hbm = pl.BlockSpec(memory_space=pltpu.HBM)
    half = pltpu.VMEM((2, 2, width // 4, width), jnp.float32)
    return pl.pallas_call(
        functools.partial(solve_kernel, p),
        out_shape=jax.ShapeDtypeStruct((width, part), jnp.float32),
        in_specs=[pl.BlockSpec(memory_space=pltpu.SMEM), hbm, hbm, vmem, vmem],
        out_specs=vmem,
        scratch_shapes=[half, half, half, pltpu.SemaphoreType.DMA((6,))],
        compiler_params=pltpu.CompilerParams(vmem_limit_bytes=24 * MIB),
        cost_estimate=pl.CostEstimate(flops=1000, bytes_accessed=1000, transcendentals=0),
        name="solve_pair",
    )(idx, packed, packed_other, r_own, r_other)


def update_kernel(p, idx, mine, other, r_own, trailing, near, far, top, bottom, out, t_buf, sems):
    x, y, core = idx[0], idx[1], idx[2]
    ny, rows, pair = t_buf.shape
    half = rows // 2
    moves = (
        (trailing.at[:, pl.ds(p * pair, pair)], t_buf.at[y]),
        (near, t_buf.at[y ^ 1]),
        (far, t_buf.at[y ^ 3]),
        (top, t_buf.at[y ^ 2, pl.ds(0, half)]),
        (bottom, t_buf.at[y ^ 2, pl.ds(half, half)]),
    )

    @pl.when(x >= p)
    def _():
        out[...] = r_own[...]

    @pl.when(x < p)
    def _():
        copies = [pltpu.make_async_copy(src, dst, sems.at[n]) for n, (src, dst) in enumerate(moves)]
        for cp in copies:
            cp.start()
        first = jnp.where(core == 0, mine[...], other[...])
        second = jnp.where(core == 0, other[...], mine[...])
        block = jnp.concatenate([first, second], axis=0)
        for cp in copies:
            cp.wait()
        step = mm(t_buf[...].reshape(ny * rows, pair), block).reshape(r_own.shape)
        out[...] = r_own[...] - step


def update(p, idx, mine, other, r_own, trailing, pieces):
    vmem = pl.BlockSpec(memory_space=pltpu.VMEM)
    hbm = pl.BlockSpec(memory_space=pltpu.HBM)
    rows, pair = pieces[0].shape
    return pl.pallas_call(
        functools.partial(update_kernel, p),
        out_shape=jax.ShapeDtypeStruct(r_own.shape, jnp.float32),
        in_specs=[pl.BlockSpec(memory_space=pltpu.SMEM), vmem, vmem, vmem] + [hbm] * 5,
        out_specs=vmem,
        scratch_shapes=[pltpu.VMEM((NY, rows, pair), jnp.float32), pltpu.SemaphoreType.DMA((5,))],
        compiler_params=pltpu.CompilerParams(vmem_limit_bytes=24 * MIB),
        cost_estimate=pl.CostEstimate(flops=1000, bytes_accessed=1000, transcendentals=0),
        name="update_rows",
    )(idx, mine, other, r_own, trailing, *pieces)


def join_kernel(groups, idx, *refs):
    y = idx[1]
    out, sems = refs[-2:]
    copies = []
    base = 0
    refs = list(refs[:-2])
    for count in groups:
        pieces, refs = refs[:count], refs[count:]
        n, height, part = pieces[0].shape
        for m, (piece, s) in enumerate(zip(pieces, (0, 1, 3, 2, 2))):
            rows = pl.ds(height // 2 if m == 4 else 0, piece.shape[1])
            columns = pl.ds(pl.multiple_of((y ^ s) * part, part), part)
            dst = out.at[pl.ds(base, n), rows, columns]
            copies.append(pltpu.make_async_copy(piece, dst, sems.at[len(copies)]))
        base += n
    for cp in copies:
        cp.start()
    for cp in copies:
        cp.wait()


def join(idx, *groups):
    n = sum(group[0].shape[0] for group in groups)
    _, height, part = groups[0][0].shape
    pieces = [piece for group in groups for piece in group]
    hbm = pl.BlockSpec(memory_space=pltpu.HBM)
    return pl.pallas_call(
        functools.partial(join_kernel, tuple(len(group) for group in groups)),
        grid=(1,),
        out_shape=jax.ShapeDtypeStruct((n, height, NY * part), jnp.float32),
        in_specs=[pl.BlockSpec(memory_space=pltpu.SMEM)] + [hbm] * len(pieces),
        out_specs=pl.BlockSpec((n, height, NY * part), lambda i: (0, 0, 0)),
        scratch_shapes=[pltpu.SemaphoreType.DMA((len(pieces),))],
        compiler_params=pltpu.CompilerParams(vmem_limit_bytes=24 * MIB),
        cost_estimate=pl.CostEstimate(flops=0, bytes_accessed=n * 3 * MIB, transcendentals=0),
        name="join_columns",
    )(idx, *pieces)


def finish_kernel(idx, own, other, c, start, *refs):
    solved, out, top, low = refs[-4:]
    i, j = pl.program_id(0), pl.program_id(1)
    height = own.shape[1]

    @pl.when(i == 0)
    def _():
        for panel in range(2):
            value = jnp.where(idx[2] == panel, own[0], other[0])
            rows = pl.ds(panel * height, height)
            solved[rows] = value
            top[j, rows], low[j, rows] = split(value)

    @pl.when(j == 0)
    def _():
        out[...] = start[...]

    a_top, a_low = split(c[0])
    out[...] -= mm3(a_top, a_low, top[j], low[j])


def finish(idx, first, own, other, blocks, start, solved):
    n, height, columns = own.shape
    rows = start.shape[0]
    pair = 2 * height
    tile = rows // 2
    hbm = pl.BlockSpec(memory_space=pltpu.HBM)

    def once(i, j):
        return jnp.where(i == 0, j, n - 1)

    block = pl.BlockSpec((1, height, columns), lambda i, j: (once(i, j), 0, 0))
    part = pl.BlockSpec((tile, columns), lambda i, j: (i, 0))
    term = pltpu.VMEM((n, pair, columns), jnp.bfloat16)
    return pl.pallas_call(
        finish_kernel,
        grid=(rows // tile, n),
        out_shape=[jax.ShapeDtypeStruct((NX * pair, columns), jnp.float32), jax.ShapeDtypeStruct(start.shape, jnp.float32)],
        in_specs=[
            pl.BlockSpec(memory_space=pltpu.SMEM),
            block,
            block,
            pl.BlockSpec((1, tile, pair), lambda i, j: (first + j, i, 0)),
            part,
        ]
        + [hbm] * len(solved),
        out_specs=[pl.BlockSpec((pair, columns), lambda i, j: (first + once(i, j), 0)), part],
        scratch_shapes=[term, term],
        input_output_aliases={5: 0} if solved else {},
        compiler_params=pltpu.CompilerParams(vmem_limit_bytes=40 * MIB),
        cost_estimate=pl.CostEstimate(
            flops=6 * n * rows * pair * columns, bytes_accessed=n * 8 * MIB, transcendentals=0
        ),
        name="finish_pairs",
    )(idx, own, other, blocks, start, *solved)


def hand_kernel(first, idx, filled, begin, end, taken, own, other, *refs):
    out, rows, sems = refs[-3:]
    before = refs[0] if len(refs) == 4 else None
    slot = pl.program_id(0)
    core = idx[2]
    n, height, _ = own.shape

    @pl.when(slot == 0)
    def _():
        copies = []
        for p in range(n):
            for k, (src, panel) in enumerate(((own, core), (other, 1 - core))):
                dst = rows.at[pl.ds(pl.multiple_of((2 * p + panel) * height, height), height)]
                copies.append(pltpu.make_async_copy(src.at[p], dst, sems.at[2 * p + k]))
        for cp in copies:
            cp.start()
        for cp in copies:
            cp.wait()

    out[...] = jnp.zeros_like(out) if before is None else before[...]

    @pl.when(filled[slot] == 1)
    def _():
        def one(i, carry):
            out[0, pl.ds(i, 1)] = rows[pl.ds(taken[slot, i] - first * 2 * height, 1)]
            return carry

        def eight(m, carry):
            for u in range(8):
                one(begin[slot] + m * 8 + u, 0)
            return carry

        whole = lax.div(end[slot] - begin[slot], 8)
        lax.fori_loop(0, whole, eight, 0)
        lax.fori_loop(begin[slot] + whole * 8, end[slot], one, 0)


def hand(first, idx, filled, begin, end, taken, own, other, before):
    slots, count = taken.shape
    n, height, columns = own.shape
    smem = pl.BlockSpec(memory_space=pltpu.SMEM)
    hbm = pl.BlockSpec(memory_space=pltpu.HBM)
    slab = pl.BlockSpec((1, count, columns), lambda i: (i, 0, 0))
    return pl.pallas_call(
        functools.partial(hand_kernel, first),
        grid=(slots,),
        out_shape=jax.ShapeDtypeStruct((slots, count, columns), jnp.float32),
        in_specs=[smem] * 5 + [hbm, hbm] + [slab] * len(before),
        out_specs=slab,
        scratch_shapes=[pltpu.VMEM((n * 2 * height, columns), jnp.float32), pltpu.SemaphoreType.DMA((2 * n,))],
        input_output_aliases={7: 0} if before else {},
        compiler_params=pltpu.CompilerParams(vmem_limit_bytes=32 * MIB),
        cost_estimate=pl.CostEstimate(flops=0, bytes_accessed=n * 4 * MIB, transcendentals=0),
        name="hand_down",
    )(idx, filled, begin, end, taken, own, other, *before)


def on_device(trailing, inverse_rows, rhs_tail, coupling, rhs_head, child_rows, owner):
    x = lax.axis_index("x")
    y = lax.axis_index("y")
    core = lax.axis_index("core")
    z = lax.axis_index("z")
    idx = jnp.stack([x, y, core, z]).astype(jnp.int32)
    rows, window = trailing.shape
    width = inverse_rows.shape[1]
    columns = rhs_tail.shape[1]
    part = columns // NY
    pair = 2 * width

    gathered = lax.all_gather(coupling, "z", axis=0, tiled=False)

    t_diag = lax.dynamic_slice(trailing, (0, pair * x + width), (rows, width))
    factors = jnp.concatenate([inverse_rows, t_diag], axis=1)
    right = rhs_tail.reshape(rows, NY, part).transpose(1, 0, 2)
    packed = jnp.concatenate([jnp.broadcast_to(factors, (NY,) + factors.shape), right], axis=2)
    packed = lax.all_to_all(packed, "y", split_axis=0, concat_axis=0, tiled=True)
    packed_other = both_cores(packed)
    r_own = packed[:, :, pair:]
    r_other = packed_other[:, :, pair:]

    chunks = {}
    after = packed
    for q in range(NX - 1, 0, -1):
        piece, _ = lax.optimization_barrier((trailing[:, q * pair : (q + 1) * pair], after))
        chunks[q] = exchange_y(piece)
        after = chunks[q][:2]

    halves = [None] * NX
    for p in range(NX - 1, -1, -1):
        mine = solve(p, idx, packed, packed_other, r_own, r_other, width)
        got = [lax.ppermute(mine, "x", [(p, (p + s) % NX)]) for s in (2, 3, 1)]
        halves[p] = jnp.where(x == p, mine, got[0] + got[1] + got[2])
        if p > 0:
            other = both_cores(halves[p])
            r_own = update(p, idx, halves[p], other, r_own, trailing, chunks[p])
            r_other = both_cores(r_own)
        if p == 2:
            first, _ = lax.optimization_barrier((halves[2:], r_own))
            first = jnp.stack(first)
            first_pieces = exchange_y(first, axis=1)
    last = jnp.stack(halves[:2])
    first_pieces, last = lax.optimization_barrier((first_pieces, last))
    last_pieces = [lax.ppermute(last, "y", [(i, i ^ s) for i in range(NY)]) for s in (2, 1, 3)]
    last_pieces = [last_pieces[n] for n in (1, 2, 0)]
    early = join(idx, (first, *first_pieces))
    early_other = both_cores(early)

    group = (x * NY + y) * NC + core
    owned = (owner == group).astype(jnp.int32)
    rank = jnp.cumsum(owned) - owned
    slot_ids = jnp.arange(SLOTS, dtype=jnp.int32)
    picked = (owned[None, :] == 1) & (rank[None, :] == slot_ids[:, None])
    rows_taken = jnp.sum(jnp.where(picked[:, :, None], child_rows[None, :, :], 0), axis=1)
    filled = jnp.any(picked, axis=1)
    filled = filled.astype(jnp.int32)
    begin = jnp.sum((rows_taken < 2 * pair).astype(jnp.int32), axis=1)
    handed = hand(2, idx, filled, begin, jnp.full_like(begin, rows_taken.shape[1]), rows_taken, early, early_other, ())

    early, early_other, handed = lax.optimization_barrier((early, early_other, handed))
    solved, remaining = finish(idx, 2, early, early_other, gathered, rhs_head, ())
    last_pieces, remaining = lax.optimization_barrier((last_pieces, remaining))
    last = join(idx, (last, *last_pieces))
    last_other = both_cores(last)
    handed = hand(0, idx, filled, jnp.zeros_like(begin), begin, rows_taken, last, last_other, (handed,))
    solved, remaining = finish(idx, 0, last, last_other, gathered, remaining, (solved,))
    return (remaining, solved, handed)


def solution(mesh):
    grid = Mesh(mesh.devices.reshape(NX, NY, NC, -1), ROW + ("z",))
    return jax.shard_map(
        on_device,
        mesh=grid,
        in_specs=(
            P(ROW, None),
            P(ROW, None),
            P(ROW, "z"),
            P(ROW, "z"),
            P(ROW, "z"),
            P(),
            P(),
        ),
        out_specs=(P(ROW, "z"), P(None, "z"), P(ROW, None, "z")),
        check_vma=False,
    )
```

```python
import functools

import jax
import jax.numpy as jnp
from jax import lax
from jax.experimental import pallas as pl
from jax.experimental.pallas import tpu as pltpu
from jax.sharding import Mesh, PartitionSpec as P

SLOTS = 4
NX, NY, NC = 4, 4, 2
ROW = ("x", "y", "core")
SWAP = [(0, 1), (1, 0)]
MIB = 1024 * 1024

def three_terms(a):
    top = a.astype(jnp.bfloat16)
    rest = a - top.astype(jnp.float32)
    mid = rest.astype(jnp.bfloat16)
    return top, mid, (rest - mid.astype(jnp.float32)).astype(jnp.bfloat16)


def mm(a, b, a_axis=1):
    n = b.shape[1]
    top, mid, low = three_terms(a)
    terms = jnp.concatenate(three_terms(b), axis=1)

    def dot(u, v):
        return lax.dot_general(u, v, (((a_axis,), (0,)), ((), ())), preferred_element_type=jnp.float32)

    first = dot(top, terms)
    second = dot(mid, terms[:, : 2 * n])
    third = dot(low, terms[:, :n])
    small = first[:, 2 * n :] + second[:, n:] + third
    return first[:, :n] + ((first[:, n : 2 * n] + second[:, :n]) + small)


def mm_t(a, b):
    return mm(a, b, 0)


def split(a):
    top = a.astype(jnp.bfloat16)
    return top, (a - top.astype(jnp.float32)).astype(jnp.bfloat16)


def mm3(a_top, a_low, b_top, b_low):
    one = functools.partial(jnp.dot, preferred_element_type=jnp.float32)
    return one(a_top, b_top) + (one(a_low, b_top) + one(a_top, b_low))


def both_cores(own):
    return lax.ppermute(own, "core", SWAP)


ONE, THREE = [[(i, i ^ s) for i in range(NY)] for s in (1, 3)]


def neighbours_y(piece):
    return lax.ppermute(piece, "y", ONE), lax.ppermute(piece, "y", THREE)


def pass_on_y(a, b, axis):
    n = a.shape[axis] // 2
    c = lax.ppermute(lax.slice_in_dim(b, 0, n, axis=axis), "y", ONE)
    d = lax.ppermute(lax.slice_in_dim(a, n, 2 * n, axis=axis), "y", THREE)
    return a, b, c, d


def exchange_y(piece, axis=0):
    return pass_on_y(*neighbours_y(piece), axis)


def solve_kernel(p, idx, fac_own, fac_other, r_own, r_other, out, g_hi, t_mid, g_low, sems):
    @pl.when(idx[0] == p)
    def _():
        width = g_hi.shape[-1]
        copies = []
        for n, (dst, y0, col) in enumerate(((g_hi, 2, 0), (t_mid, 0, width), (g_low, 0, 0))):
            for j, fac in enumerate((fac_own, fac_other)):
                src = fac.at[pl.ds(y0, 2), :, pl.ds(col, width)]
                cp = pltpu.make_async_copy(src, dst.at[j], sems.at[2 * n + j])
                cp.start()
                copies.append(cp)

        def rows(y0):
            a = r_own[pl.ds(y0, 2)]
            b = r_other[pl.ds(y0, 2)]
            return jnp.concatenate([a.reshape(-1, a.shape[-1]), b.reshape(-1, b.shape[-1])], axis=0)

        r_hi, r_low = rows(2), rows(0)
        copies[0].wait()
        copies[1].wait()
        x_hi = mm_t(g_hi[...].reshape(width, width), r_hi)
        copies[2].wait()
        copies[3].wait()
        r_low = r_low - mm(t_mid[...].reshape(width, width), x_hi)
        copies[4].wait()
        copies[5].wait()
        x_low = mm_t(g_low[...].reshape(width, width), r_low)
        out[...] = jnp.where(idx[2] == 0, x_low, x_hi)


def solve(p, idx, packed, packed_other, r_own, r_other, width):
    part = r_own.shape[-1]
    vmem = pl.BlockSpec(memory_space=pltpu.VMEM)
    hbm = pl.BlockSpec(memory_space=pltpu.HBM)
    half = pltpu.VMEM((2, 2, width // 4, width), jnp.float32)
    return pl.pallas_call(
        functools.partial(solve_kernel, p),
        out_shape=jax.ShapeDtypeStruct((width, part), jnp.float32),
        in_specs=[pl.BlockSpec(memory_space=pltpu.SMEM), hbm, hbm, vmem, vmem],
        out_specs=vmem,
        scratch_shapes=[half, half, half, pltpu.SemaphoreType.DMA((6,))],
        compiler_params=pltpu.CompilerParams(vmem_limit_bytes=16 * MIB),
        cost_estimate=pl.CostEstimate(flops=1000, bytes_accessed=1000, transcendentals=0),
        name="solve_pair",
    )(idx, packed, packed_other, r_own, r_other)


def update_kernel(p, idx, mine, other, r_own, trailing, near, far, top, bottom, out, t_buf, sems):
    x, y, core = idx[0], idx[1], idx[2]
    ny, rows, pair = t_buf.shape
    half = rows // 2
    moves = (
        (trailing.at[:, pl.ds(p * pair, pair)], t_buf.at[y]),
        (near, t_buf.at[y ^ 1]),
        (far, t_buf.at[y ^ 3]),
        (top, t_buf.at[y ^ 2, pl.ds(0, half)]),
        (bottom, t_buf.at[y ^ 2, pl.ds(half, half)]),
    )

    @pl.when(x >= p)
    def _():
        out[...] = r_own[...]

    @pl.when(x < p)
    def _():
        copies = [pltpu.make_async_copy(src, dst, sems.at[n]) for n, (src, dst) in enumerate(moves)]
        for cp in copies:
            cp.start()
        first = jnp.where(core == 0, mine[...], other[...])
        second = jnp.where(core == 0, other[...], mine[...])
        block = jnp.concatenate([first, second], axis=0)
        for cp in copies:
            cp.wait()
        step = mm(t_buf[...].reshape(ny * rows, pair), block).reshape(r_own.shape)
        out[...] = r_own[...] - step


def update(p, idx, mine, other, r_own, trailing, pieces):
    vmem = pl.BlockSpec(memory_space=pltpu.VMEM)
    hbm = pl.BlockSpec(memory_space=pltpu.HBM)
    rows, pair = pieces[0].shape
    return pl.pallas_call(
        functools.partial(update_kernel, p),
        out_shape=jax.ShapeDtypeStruct(r_own.shape, jnp.float32),
        in_specs=[pl.BlockSpec(memory_space=pltpu.SMEM), vmem, vmem, vmem] + [hbm] * 5,
        out_specs=vmem,
        scratch_shapes=[pltpu.VMEM((NY, rows, pair), jnp.float32), pltpu.SemaphoreType.DMA((5,))],
        compiler_params=pltpu.CompilerParams(vmem_limit_bytes=16 * MIB),
        cost_estimate=pl.CostEstimate(flops=1000, bytes_accessed=1000, transcendentals=0),
        name="update_rows",
    )(idx, mine, other, r_own, trailing, *pieces)


def join_kernel(groups, idx, *refs):
    y = idx[1]
    out, sems = refs[-2:]
    copies = []
    base = 0
    refs = list(refs[:-2])
    for count in groups:
        pieces, refs = refs[:count], refs[count:]
        n, height, part = pieces[0].shape
        for m, (piece, s) in enumerate(zip(pieces, (0, 1, 3, 2, 2))):
            rows = pl.ds(height // 2 if m == 4 else 0, piece.shape[1])
            columns = pl.ds(pl.multiple_of((y ^ s) * part, part), part)
            dst = out.at[pl.ds(base, n), rows, columns]
            copies.append(pltpu.make_async_copy(piece, dst, sems.at[len(copies)]))
        base += n
    for cp in copies:
        cp.start()
    for cp in copies:
        cp.wait()


def join(idx, *groups):
    n = sum(group[0].shape[0] for group in groups)
    _, height, part = groups[0][0].shape
    pieces = [piece for group in groups for piece in group]
    hbm = pl.BlockSpec(memory_space=pltpu.HBM)
    return pl.pallas_call(
        functools.partial(join_kernel, tuple(len(group) for group in groups)),
        grid=(1,),
        out_shape=jax.ShapeDtypeStruct((n, height, NY * part), jnp.float32),
        in_specs=[pl.BlockSpec(memory_space=pltpu.SMEM)] + [hbm] * len(pieces),
        out_specs=pl.BlockSpec((n, height, NY * part), lambda i: (0, 0, 0)),
        scratch_shapes=[pltpu.SemaphoreType.DMA((len(pieces),))],
        compiler_params=pltpu.CompilerParams(vmem_limit_bytes=12 * MIB),
        cost_estimate=pl.CostEstimate(flops=0, bytes_accessed=n * 3 * MIB, transcendentals=0),
        name="join_columns",
    )(idx, *pieces)


def finish_kernel(count, idx, own, other, c, *refs):
    starts = refs[:count]
    solved, out, top, low = refs[-4:]
    i, j = pl.program_id(0), pl.program_id(1)
    height = own.shape[1]

    @pl.when(i == 0)
    def _():
        for panel in range(2):
            value = jnp.where(idx[2] == panel, own[0], other[0])
            rows = pl.ds(panel * height, height)
            solved[rows] = value
            top[j, rows], low[j, rows] = split(value)

    @pl.when(j == 0)
    def _():
        out[...] = sum((start[...] for start in starts), jnp.zeros_like(out))

    a_top, a_low = split(c[0])
    out[...] -= mm3(a_top, a_low, top[j], low[j])


def finish(idx, first, own, other, blocks, starts, solved):
    n, height, columns = own.shape
    rows = blocks.shape[1]
    pair = 2 * height
    tile = rows // 2
    hbm = pl.BlockSpec(memory_space=pltpu.HBM)

    def once(i, j):
        return jnp.where(i == 0, j, n - 1)

    block = pl.BlockSpec((1, height, columns), lambda i, j: (once(i, j), 0, 0))
    part = pl.BlockSpec((tile, columns), lambda i, j: (i, 0))
    term = pltpu.VMEM((n, pair, columns), jnp.bfloat16)
    return pl.pallas_call(
        functools.partial(finish_kernel, len(starts)),
        grid=(rows // tile, n),
        out_shape=[jax.ShapeDtypeStruct((NX * pair, columns), jnp.float32), jax.ShapeDtypeStruct((rows, columns), jnp.float32)],
        in_specs=[
            pl.BlockSpec(memory_space=pltpu.SMEM),
            block,
            block,
            pl.BlockSpec((1, tile, pair), lambda i, j: (first + j, i, 0)),
        ]
        + [part] * len(starts)
        + [hbm] * len(solved),
        out_specs=[pl.BlockSpec((pair, columns), lambda i, j: (first + once(i, j), 0)), part],
        scratch_shapes=[term, term],
        input_output_aliases={4 + len(starts): 0} if solved else {},
        compiler_params=pltpu.CompilerParams(vmem_limit_bytes=34 * MIB),
        cost_estimate=pl.CostEstimate(
            flops=6 * n * rows * pair * columns, bytes_accessed=n * 8 * MIB, transcendentals=0
        ),
        name="finish_pairs",
    )(idx, own, other, blocks, *starts, *solved)


def hand_kernel(first, idx, filled, begin, end, taken, own, other, *refs):
    out, rows, sems = refs[-3:]
    before = refs[0] if len(refs) == 4 else None
    slot = pl.program_id(0)
    core = idx[2]
    n, height, _ = own.shape

    @pl.when(slot == 0)
    def _():
        copies = []
        for p in range(n):
            for k, (src, panel) in enumerate(((own, core), (other, 1 - core))):
                dst = rows.at[pl.ds(pl.multiple_of((2 * p + panel) * height, height), height)]
                copies.append(pltpu.make_async_copy(src.at[p], dst, sems.at[2 * p + k]))
        for cp in copies:
            cp.start()
        for cp in copies:
            cp.wait()

    out[...] = jnp.zeros_like(out) if before is None else before[...]

    @pl.when(filled[slot] == 1)
    def _():
        def one(i, carry):
            out[0, pl.ds(i, 1)] = rows[pl.ds(taken[slot, i] - first * 2 * height, 1)]
            return carry

        def eight(m, carry):
            for u in range(8):
                one(begin[slot] + m * 8 + u, 0)
            return carry

        whole = lax.div(end[slot] - begin[slot], 8)
        lax.fori_loop(0, whole, eight, 0)
        lax.fori_loop(begin[slot] + whole * 8, end[slot], one, 0)


def hand(first, idx, filled, begin, end, taken, own, other, before):
    slots, count = taken.shape
    n, height, columns = own.shape
    smem = pl.BlockSpec(memory_space=pltpu.SMEM)
    hbm = pl.BlockSpec(memory_space=pltpu.HBM)
    slab = pl.BlockSpec((1, count, columns), lambda i: (i, 0, 0))
    return pl.pallas_call(
        functools.partial(hand_kernel, first),
        grid=(slots,),
        out_shape=jax.ShapeDtypeStruct((slots, count, columns), jnp.float32),
        in_specs=[smem] * 5 + [hbm, hbm] + [slab] * len(before),
        out_specs=slab,
        scratch_shapes=[pltpu.VMEM((n * 2 * height, columns), jnp.float32), pltpu.SemaphoreType.DMA((2 * n,))],
        input_output_aliases={7: 0} if before else {},
        compiler_params=pltpu.CompilerParams(vmem_limit_bytes=16 * MIB),
        cost_estimate=pl.CostEstimate(flops=0, bytes_accessed=n * 4 * MIB, transcendentals=0),
        name="hand_down",
    )(idx, filled, begin, end, taken, own, other, *before)


def on_device(trailing, inverse_rows, rhs_tail, coupling, rhs_head, child_rows, owner):
    x = lax.axis_index("x")
    y = lax.axis_index("y")
    core = lax.axis_index("core")
    z = lax.axis_index("z")
    idx = jnp.stack([x, y, core, z]).astype(jnp.int32)
    rows, window = trailing.shape
    width = inverse_rows.shape[1]
    columns = rhs_tail.shape[1]
    part = columns // NY
    pair = 2 * width

    gathered = lax.all_gather(coupling, "z", axis=0, tiled=False)

    t_diag = lax.dynamic_slice(trailing, (0, pair * x + width), (rows, width))
    factors = jnp.concatenate([inverse_rows, t_diag], axis=1)
    right = rhs_tail.reshape(rows, NY, part).transpose(1, 0, 2)
    packed = jnp.concatenate([jnp.broadcast_to(factors, (NY,) + factors.shape), right], axis=2)
    packed = lax.all_to_all(packed, "y", split_axis=0, concat_axis=0, tiled=True)
    packed_other = both_cores(packed)
    r_own = packed[:, :, pair:]
    r_other = packed_other[:, :, pair:]

    chunks = {}
    after = packed
    for q in range(NX - 1, 0, -1):
        piece, _ = lax.optimization_barrier((trailing[:, q * pair : (q + 1) * pair], after))
        chunks[q] = exchange_y(piece)
        after = chunks[q][:2]

    halves = [None] * NX
    for p in range(NX - 1, -1, -1):
        mine = solve(p, idx, packed, packed_other, r_own, r_other, width)
        got = [lax.ppermute(mine, "x", [(p, (p + s) % NX)]) for s in (2, 3, 1)]
        halves[p] = jnp.where(x == p, mine, got[0] + got[1] + got[2])
        if p > 0:
            other = both_cores(halves[p])
            r_own = update(p, idx, halves[p], other, r_own, trailing, chunks[p])
            r_other = both_cores(r_own)
        if p == 2:
            first, _ = lax.optimization_barrier((halves[2:], r_own))
            first = jnp.stack(first)
            first_pieces = exchange_y(first, axis=1)
    last = jnp.stack(halves[:2])
    first_pieces, last = lax.optimization_barrier((first_pieces, last))
    last_pieces = [lax.ppermute(last, "y", [(i, i ^ s) for i in range(NY)]) for s in (2, 1, 3)]
    last_pieces = [last_pieces[n] for n in (1, 2, 0)]
    early = join(idx, (first, *first_pieces))
    early_other = both_cores(early)

    group = (x * NY + y) * NC + core
    owned = (owner == group).astype(jnp.int32)
    rank = jnp.cumsum(owned) - owned
    slot_ids = jnp.arange(SLOTS, dtype=jnp.int32)
    picked = (owned[None, :] == 1) & (rank[None, :] == slot_ids[:, None])
    rows_taken = jnp.sum(jnp.where(picked[:, :, None], child_rows[None, :, :], 0), axis=1)
    filled = jnp.any(picked, axis=1)
    filled = filled.astype(jnp.int32)
    begin = jnp.sum((rows_taken < 2 * pair).astype(jnp.int32), axis=1)
    handed = hand(2, idx, filled, begin, jnp.full_like(begin, rows_taken.shape[1]), rows_taken, early, early_other, ())

    early, early_other, handed = lax.optimization_barrier((early, early_other, handed))
    solved, remaining = finish(idx, 2, early, early_other, gathered, (), ())
    last_pieces, remaining = lax.optimization_barrier((last_pieces, remaining))
    last_other = [both_cores(piece) for piece in (last, *last_pieces)]
    last = join(idx, (last, *last_pieces))
    last_other = join(idx, last_other)
    handed = hand(0, idx, filled, jnp.zeros_like(begin), begin, rows_taken, last, last_other, (handed,))
    solved, remaining = finish(idx, 0, last, last_other, gathered, (rhs_head, remaining), (solved,))
    return (remaining, solved, handed)


def solution(mesh):
    grid = Mesh(mesh.devices.reshape(NX, NY, NC, -1), ROW + ("z",))
    return jax.shard_map(
        on_device,
        mesh=grid,
        in_specs=(
            P(ROW, None),
            P(ROW, None),
            P(ROW, "z"),
            P(ROW, "z"),
            P(ROW, "z"),
            P(),
            P(),
        ),
        out_specs=(P(ROW, "z"), P(None, "z"), P(ROW, None, "z")),
        check_vma=False,
    )
```

```python
import functools

import jax
import jax.numpy as jnp
from jax import lax
from jax.experimental import pallas as pl
from jax.experimental.pallas import tpu as pltpu
from jax.sharding import Mesh, PartitionSpec as P

SLOTS = 4
NX, NY, NC = 4, 4, 2
ROW = ("x", "y", "core")
SWAP = [(0, 1), (1, 0)]
MIB = 1024 * 1024

def three_terms(a):
    top = a.astype(jnp.bfloat16)
    rest = a - top.astype(jnp.float32)
    mid = rest.astype(jnp.bfloat16)
    return top, mid, (rest - mid.astype(jnp.float32)).astype(jnp.bfloat16)


def mm(a, b, a_axis=1):
    n = b.shape[1]
    top, mid, low = three_terms(a)
    terms = jnp.concatenate(three_terms(b), axis=1)

    def dot(u, v):
        return lax.dot_general(u, v, (((a_axis,), (0,)), ((), ())), preferred_element_type=jnp.float32)

    first = dot(top, terms)
    second = dot(mid, terms[:, : 2 * n])
    third = dot(low, terms[:, :n])
    small = first[:, 2 * n :] + second[:, n:] + third
    return first[:, :n] + ((first[:, n : 2 * n] + second[:, :n]) + small)


def mm_t(a, b):
    return mm(a, b, 0)


def split(a):
    top = a.astype(jnp.bfloat16)
    return top, (a - top.astype(jnp.float32)).astype(jnp.bfloat16)


def mm3(a_top, a_low, b_top, b_low):
    one = functools.partial(jnp.dot, preferred_element_type=jnp.float32)
    return one(a_top, b_top) + (one(a_low, b_top) + one(a_top, b_low))


def both_cores(own):
    return lax.ppermute(own, "core", SWAP)


ONE, THREE = [[(i, i ^ s) for i in range(NY)] for s in (1, 3)]


def neighbours_y(piece):
    return lax.ppermute(piece, "y", ONE), lax.ppermute(piece, "y", THREE)


def pass_on_y(a, b, axis):
    n = a.shape[axis] // 2
    c = lax.ppermute(lax.slice_in_dim(b, 0, n, axis=axis), "y", ONE)
    d = lax.ppermute(lax.slice_in_dim(a, n, 2 * n, axis=axis), "y", THREE)
    return a, b, c, d


def exchange_y(piece, axis=0):
    return pass_on_y(*neighbours_y(piece), axis)


def solve_kernel(p, idx, fac_own, fac_other, r_own, r_other, out, g_hi, t_mid, g_low, sems):
    @pl.when(idx[0] == p)
    def _():
        width = g_hi.shape[-1]
        copies = []
        for n, (dst, y0, col) in enumerate(((g_hi, 2, 0), (t_mid, 0, width), (g_low, 0, 0))):
            for j, fac in enumerate((fac_own, fac_other)):
                src = fac.at[pl.ds(y0, 2), :, pl.ds(col, width)]
                cp = pltpu.make_async_copy(src, dst.at[j], sems.at[2 * n + j])
                cp.start()
                copies.append(cp)

        def rows(y0):
            a = r_own[pl.ds(y0, 2)]
            b = r_other[pl.ds(y0, 2)]
            return jnp.concatenate([a.reshape(-1, a.shape[-1]), b.reshape(-1, b.shape[-1])], axis=0)

        r_hi, r_low = rows(2), rows(0)
        copies[0].wait()
        copies[1].wait()
        x_hi = mm_t(g_hi[...].reshape(width, width), r_hi)
        copies[2].wait()
        copies[3].wait()
        r_low = r_low - mm(t_mid[...].reshape(width, width), x_hi)
        copies[4].wait()
        copies[5].wait()
        x_low = mm_t(g_low[...].reshape(width, width), r_low)
        out[...] = jnp.where(idx[2] == 0, x_low, x_hi)


def solve(p, idx, packed, packed_other, r_own, r_other, width):
    part = r_own.shape[-1]
    vmem = pl.BlockSpec(memory_space=pltpu.VMEM)
    hbm = pl.BlockSpec(memory_space=pltpu.HBM)
    half = pltpu.VMEM((2, 2, width // 4, width), jnp.float32)
    return pl.pallas_call(
        functools.partial(solve_kernel, p),
        out_shape=jax.ShapeDtypeStruct((width, part), jnp.float32),
        in_specs=[pl.BlockSpec(memory_space=pltpu.SMEM), hbm, hbm, vmem, vmem],
        out_specs=vmem,
        scratch_shapes=[half, half, half, pltpu.SemaphoreType.DMA((6,))],
        compiler_params=pltpu.CompilerParams(vmem_limit_bytes=16 * MIB),
        cost_estimate=pl.CostEstimate(flops=1000, bytes_accessed=1000, transcendentals=0),
        name="solve_pair",
    )(idx, packed, packed_other, r_own, r_other)


def update_kernel(p, idx, mine, other, r_own, trailing, near, far, top, bottom, out, t_buf, sems):
    x, y, core = idx[0], idx[1], idx[2]
    ny, rows, pair = t_buf.shape
    half = rows // 2
    moves = (
        (trailing.at[:, pl.ds(p * pair, pair)], t_buf.at[y]),
        (near, t_buf.at[y ^ 1]),
        (far, t_buf.at[y ^ 3]),
        (top, t_buf.at[y ^ 2, pl.ds(0, half)]),
        (bottom, t_buf.at[y ^ 2, pl.ds(half, half)]),
    )

    @pl.when(x >= p)
    def _():
        out[...] = r_own[...]

    @pl.when(x < p)
    def _():
        copies = [pltpu.make_async_copy(src, dst, sems.at[n]) for n, (src, dst) in enumerate(moves)]
        for cp in copies:
            cp.start()
        first = jnp.where(core == 0, mine[...], other[...])
        second = jnp.where(core == 0, other[...], mine[...])
        block = jnp.concatenate([first, second], axis=0)
        for cp in copies:
            cp.wait()
        step = mm(t_buf[...].reshape(ny * rows, pair), block).reshape(r_own.shape)
        out[...] = r_own[...] - step


def update(p, idx, mine, other, r_own, trailing, pieces):
    vmem = pl.BlockSpec(memory_space=pltpu.VMEM)
    hbm = pl.BlockSpec(memory_space=pltpu.HBM)
    rows, pair = pieces[0].shape
    return pl.pallas_call(
        functools.partial(update_kernel, p),
        out_shape=jax.ShapeDtypeStruct(r_own.shape, jnp.float32),
        in_specs=[pl.BlockSpec(memory_space=pltpu.SMEM), vmem, vmem, vmem] + [hbm] * 5,
        out_specs=vmem,
        scratch_shapes=[pltpu.VMEM((NY, rows, pair), jnp.float32), pltpu.SemaphoreType.DMA((5,))],
        compiler_params=pltpu.CompilerParams(vmem_limit_bytes=16 * MIB),
        cost_estimate=pl.CostEstimate(flops=1000, bytes_accessed=1000, transcendentals=0),
        name="update_rows",
    )(idx, mine, other, r_own, trailing, *pieces)


def join_kernel(groups, idx, *refs):
    y = idx[1]
    out, sems = refs[-2:]
    copies = []
    base = 0
    refs = list(refs[:-2])
    for count in groups:
        pieces, refs = refs[:count], refs[count:]
        n, height, part = pieces[0].shape
        for m, (piece, s) in enumerate(zip(pieces, (0, 1, 3, 2, 2))):
            rows = pl.ds(height // 2 if m == 4 else 0, piece.shape[1])
            columns = pl.ds(pl.multiple_of((y ^ s) * part, part), part)
            dst = out.at[pl.ds(base, n), rows, columns]
            copies.append(pltpu.make_async_copy(piece, dst, sems.at[len(copies)]))
        base += n
    for cp in copies:
        cp.start()
    for cp in copies:
        cp.wait()


def join(idx, *groups):
    n = sum(group[0].shape[0] for group in groups)
    _, height, part = groups[0][0].shape
    pieces = [piece for group in groups for piece in group]
    hbm = pl.BlockSpec(memory_space=pltpu.HBM)
    return pl.pallas_call(
        functools.partial(join_kernel, tuple(len(group) for group in groups)),
        grid=(1,),
        out_shape=jax.ShapeDtypeStruct((n, height, NY * part), jnp.float32),
        in_specs=[pl.BlockSpec(memory_space=pltpu.SMEM)] + [hbm] * len(pieces),
        out_specs=pl.BlockSpec((n, height, NY * part), lambda i: (0, 0, 0)),
        scratch_shapes=[pltpu.SemaphoreType.DMA((len(pieces),))],
        compiler_params=pltpu.CompilerParams(vmem_limit_bytes=12 * MIB),
        cost_estimate=pl.CostEstimate(flops=0, bytes_accessed=n * 3 * MIB, transcendentals=0),
        name="join_columns",
    )(idx, *pieces)


def finish_kernel(count, idx, own, other, c, *refs):
    starts = refs[:count]
    solved, out, top, low = refs[-4:]
    i, j = pl.program_id(0), pl.program_id(1)
    height = own.shape[1]

    @pl.when(i == 0)
    def _():
        for panel in range(2):
            value = jnp.where(idx[2] == panel, own[0], other[0])
            rows = pl.ds(panel * height, height)
            solved[rows] = value
            top[j, rows], low[j, rows] = split(value)

    @pl.when(j == 0)
    def _():
        out[...] = sum((start[...] for start in starts), jnp.zeros_like(out))

    a_top, a_low = split(c[0])
    out[...] -= mm3(a_top, a_low, top[j], low[j])


def finish(idx, first, own, other, blocks, starts, solved):
    n, height, columns = own.shape
    rows = blocks.shape[1]
    pair = 2 * height
    tile = rows // 2
    hbm = pl.BlockSpec(memory_space=pltpu.HBM)

    def once(i, j):
        return jnp.where(i == 0, j, n - 1)

    block = pl.BlockSpec((1, height, columns), lambda i, j: (once(i, j), 0, 0))
    part = pl.BlockSpec((tile, columns), lambda i, j: (i, 0))
    term = pltpu.VMEM((n, pair, columns), jnp.bfloat16)
    return pl.pallas_call(
        functools.partial(finish_kernel, len(starts)),
        grid=(rows // tile, n),
        out_shape=[jax.ShapeDtypeStruct((NX * pair, columns), jnp.float32), jax.ShapeDtypeStruct((rows, columns), jnp.float32)],
        in_specs=[
            pl.BlockSpec(memory_space=pltpu.SMEM),
            block,
            block,
            pl.BlockSpec((1, tile, pair), lambda i, j: (first + j, i, 0)),
        ]
        + [part] * len(starts)
        + [hbm] * len(solved),
        out_specs=[pl.BlockSpec((pair, columns), lambda i, j: (first + once(i, j), 0)), part],
        scratch_shapes=[term, term],
        input_output_aliases={4 + len(starts): 0} if solved else {},
        compiler_params=pltpu.CompilerParams(vmem_limit_bytes=34 * MIB),
        cost_estimate=pl.CostEstimate(
            flops=6 * n * rows * pair * columns, bytes_accessed=n * 8 * MIB, transcendentals=0
        ),
        name="finish_pairs",
    )(idx, own, other, blocks, *starts, *solved)


def hand_kernel(first, idx, filled, begin, end, taken, own, other, *refs):
    out, rows, sems = refs[-3:]
    before = refs[0] if len(refs) == 4 else None
    slot = pl.program_id(0)
    core = idx[2]
    n, height, _ = own.shape

    @pl.when(slot == 0)
    def _():
        copies = []
        for p in range(n):
            for k, (src, panel) in enumerate(((own, core), (other, 1 - core))):
                dst = rows.at[pl.ds(pl.multiple_of((2 * p + panel) * height, height), height)]
                copies.append(pltpu.make_async_copy(src.at[p], dst, sems.at[2 * p + k]))
        for cp in copies:
            cp.start()
        for cp in copies:
            cp.wait()

    out[...] = jnp.zeros_like(out) if before is None else before[...]

    @pl.when(filled[slot] == 1)
    def _():
        def one(i, carry):
            out[0, pl.ds(i, 1)] = rows[pl.ds(taken[slot, i] - first * 2 * height, 1)]
            return carry

        def sixteen(m, carry):
            places = [begin[slot] + m * 16 + u for u in range(16)]
            found = [rows[pl.ds(taken[slot, i] - first * 2 * height, 1)] for i in places]
            for i, row in zip(places, found):
                out[0, pl.ds(i, 1)] = row
            return carry

        whole = lax.div(end[slot] - begin[slot], 16)
        lax.fori_loop(0, whole, sixteen, 0)
        lax.fori_loop(begin[slot] + whole * 16, end[slot], one, 0)


def hand(first, idx, filled, begin, end, taken, own, other, before):
    slots, count = taken.shape
    n, height, columns = own.shape
    smem = pl.BlockSpec(memory_space=pltpu.SMEM)
    hbm = pl.BlockSpec(memory_space=pltpu.HBM)
    slab = pl.BlockSpec((1, count, columns), lambda i: (i, 0, 0))
    return pl.pallas_call(
        functools.partial(hand_kernel, first),
        grid=(slots,),
        out_shape=jax.ShapeDtypeStruct((slots, count, columns), jnp.float32),
        in_specs=[smem] * 5 + [hbm, hbm] + [slab] * len(before),
        out_specs=slab,
        scratch_shapes=[pltpu.VMEM((n * 2 * height, columns), jnp.float32), pltpu.SemaphoreType.DMA((2 * n,))],
        input_output_aliases={7: 0} if before else {},
        compiler_params=pltpu.CompilerParams(vmem_limit_bytes=16 * MIB),
        cost_estimate=pl.CostEstimate(flops=0, bytes_accessed=n * 4 * MIB, transcendentals=0),
        name="hand_down",
    )(idx, filled, begin, end, taken, own, other, *before)


def on_device(trailing, inverse_rows, rhs_tail, coupling, rhs_head, child_rows, owner):
    x = lax.axis_index("x")
    y = lax.axis_index("y")
    core = lax.axis_index("core")
    z = lax.axis_index("z")
    idx = jnp.stack([x, y, core, z]).astype(jnp.int32)
    rows, window = trailing.shape
    width = inverse_rows.shape[1]
    columns = rhs_tail.shape[1]
    part = columns // NY
    pair = 2 * width

    gathered = lax.all_gather(coupling, "z", axis=0, tiled=False)

    t_diag = lax.dynamic_slice(trailing, (0, pair * x + width), (rows, width))
    factors = jnp.concatenate([inverse_rows, t_diag], axis=1)
    right = rhs_tail.reshape(rows, NY, part).transpose(1, 0, 2)
    packed = jnp.concatenate([jnp.broadcast_to(factors, (NY,) + factors.shape), right], axis=2)
    packed = lax.all_to_all(packed, "y", split_axis=0, concat_axis=0, tiled=True)
    packed_other = both_cores(packed)
    r_own = packed[:, :, pair:]
    r_other = packed_other[:, :, pair:]

    chunks = {}
    after = packed
    for q in range(NX - 1, 0, -1):
        piece, _ = lax.optimization_barrier((trailing[:, q * pair : (q + 1) * pair], after))
        chunks[q] = exchange_y(piece)
        after = chunks[q][:2]

    halves = [None] * NX
    for p in range(NX - 1, -1, -1):
        mine = solve(p, idx, packed, packed_other, r_own, r_other, width)
        got = [lax.ppermute(mine, "x", [(p, (p + s) % NX)]) for s in (2, 3, 1)]
        halves[p] = jnp.where(x == p, mine, got[0] + got[1] + got[2])
        if p > 0:
            other = both_cores(halves[p])
            r_own = update(p, idx, halves[p], other, r_own, trailing, chunks[p])
            r_other = both_cores(r_own)
        if p == 2:
            first, _ = lax.optimization_barrier((halves[2:], r_own))
            first = jnp.stack(first)
            first_pieces = exchange_y(first, axis=1)
    last = jnp.stack(halves[:2])
    first_pieces, last = lax.optimization_barrier((first_pieces, last))
    last_pieces = [lax.ppermute(last, "y", [(i, i ^ s) for i in range(NY)]) for s in (2, 1, 3)]
    last_pieces = [last_pieces[n] for n in (1, 2, 0)]
    early = join(idx, (first, *first_pieces))
    early_other = both_cores(early)

    group = (x * NY + y) * NC + core
    owned = (owner == group).astype(jnp.int32)
    rank = jnp.cumsum(owned) - owned
    slot_ids = jnp.arange(SLOTS, dtype=jnp.int32)
    picked = (owned[None, :] == 1) & (rank[None, :] == slot_ids[:, None])
    rows_taken = jnp.sum(jnp.where(picked[:, :, None], child_rows[None, :, :], 0), axis=1)
    filled = jnp.any(picked, axis=1)
    filled = filled.astype(jnp.int32)
    begin = jnp.sum((rows_taken < 2 * pair).astype(jnp.int32), axis=1)
    handed = hand(2, idx, filled, begin, jnp.full_like(begin, rows_taken.shape[1]), rows_taken, early, early_other, ())

    early, early_other, handed = lax.optimization_barrier((early, early_other, handed))
    solved, remaining = finish(idx, 2, early, early_other, gathered, (), ())
    last_pieces, remaining = lax.optimization_barrier((last_pieces, remaining))
    last_other = [both_cores(piece) for piece in (last, *last_pieces)]
    last = join(idx, (last, *last_pieces))
    last_other = join(idx, last_other)
    handed = hand(0, idx, filled, jnp.zeros_like(begin), begin, rows_taken, last, last_other, (handed,))
    solved, remaining = finish(idx, 0, last, last_other, gathered, (rhs_head, remaining), (solved,))
    return (remaining, solved, handed)


def solution(mesh):
    grid = Mesh(mesh.devices.reshape(NX, NY, NC, -1), ROW + ("z",))
    return jax.shard_map(
        on_device,
        mesh=grid,
        in_specs=(
            P(ROW, None),
            P(ROW, None),
            P(ROW, "z"),
            P(ROW, "z"),
            P(ROW, "z"),
            P(),
            P(),
        ),
        out_specs=(P(ROW, "z"), P(None, "z"), P(ROW, None, "z")),
        check_vma=False,
    )
```
